512 devices in a mesh: ctx: 64 (over z_hi, x, y, core), tp: 8 (over z_lo).
Axes of the slice: x: 4, y: 4, z: 16 (z_hi: 2, z_lo: 8; z = z_hi * 8 + z_lo), core: 2. Of those that a mesh axis runs over, the one named last changes fastest.
Arguments:
- queries: bfloat16 [8192, 8192], P('ctx', 'tp'), may hold values from -8 to 8
- keys: bfloat16 [8192, 1024], P('ctx', 'tp'), may hold values from -8 to 8
- values: bfloat16 [8192, 1024], P('ctx', 'tp'), may hold values from -6 to 6
- out_weight: bfloat16 [4096, 8192], P('ctx', 'tp'), may hold values from -0.29882812 to 0.29882812
Outputs:
- mixed_out: bfloat16 [8192, 4096], P('ctx', 'tp')
The draws below stay inside these ranges and needn't reach their ends.
All inputs are finite; a program needn't handle non-finite values.
Results may differ from the reference program's by a relative error of at most 0.012.
Values may be sent and summed in bfloat16 or wider, within the bound.
A program may use at most 128 MiB of HBM per device.

```python
import math
import jax
import jax.numpy as jnp
from jax import lax

S_DEV = 128
H = 64
KVH = 8
HD = 128
DM = 4096
S_TOT = 8192
N_CTX = 64


def draw_queries(key, part):
    key = jax.random.fold_in(key, 11)
    full_shape = (S_TOT, KVH, H // KVH, HD)
    drawn = jax.random.truncated_normal(key, -6.0, 6.0, full_shape, jnp.float32)
    return drawn.reshape(S_TOT, H * HD).astype(jnp.bfloat16)


def draw_keys(key, part):
    key = jax.random.fold_in(key, 23)
    full_shape = (S_TOT, KVH, HD)
    drawn = jax.random.truncated_normal(key, -6.0, 6.0, full_shape, jnp.float32)
    return drawn.reshape(S_TOT, KVH * HD).astype(jnp.bfloat16)


def steps_of(key, shape, cuts, low, largest):
    loudness, own = 1.0, jax.random.fold_in(key, 6)
    for position, parts in cuts:
        steps = jnp.exp(jax.random.uniform(jax.random.fold_in(own, position), (parts,), jnp.float32, low / len(cuts), largest / len(cuts)))
        loudness = loudness * jnp.repeat(steps, shape[position] // parts).reshape([-1 if axis == position else 1 for axis in range(len(shape))])
    return loudness


def scatter_about(key, shape, deviation, most, split=(), kind=jnp.bfloat16):
    gain = steps_of(key, shape, split, -0.22, 0.18) if split else 1.0
    values = jax.random.normal(key, shape, jnp.float32) * deviation * gain
    return jnp.minimum(jnp.maximum(values, -most), most).astype(kind)


def setup_inputs(seed: int = 0) -> dict:
    splits = jax.random.split(jax.random.key(seed), 5)
    queries = draw_queries(jax.random.fold_in(splits[4], 71), 0)
    keys = draw_keys(jax.random.fold_in(splits[4], 71), 0)
    values = scatter_about(splits[2], (S_TOT, KVH * HD), 1.0, 6.0, ((0, 64), (1, 8)))
    out_weight = scatter_about(splits[3], (DM, H * HD), 0.05, 0.29882812, ((0, 64), (1, 8)))
    return {"queries": queries, "keys": keys, "values": values, "out_weight": out_weight}


def reference(queries, keys, values, out_weight):
    sequence = S_DEV * N_CTX
    repeat = H // KVH
    block_rows = math.gcd(sequence, 128)
    n_blocks = sequence // block_rows
    score_scale = 1.0 / math.sqrt(HD)
    positions = jnp.arange(sequence, dtype=jnp.int32)
    grouped = queries.reshape(n_blocks, block_rows, KVH, repeat, HD)
    key_heads = keys.reshape(sequence, KVH, HD).astype(jnp.float32)
    value_heads = values.reshape(sequence, KVH, HD).astype(jnp.float32)
    starts = (jnp.arange(n_blocks, dtype=jnp.int32) * block_rows).astype(jnp.int32)

    def one_block(inputs):
        query_block, first_row = inputs
        scores = jnp.einsum('sgrd,kgd->sgrk', query_block.astype(jnp.float32), key_heads) * score_scale
        query_places = first_row + jnp.arange(block_rows, dtype=jnp.int32)
        allowed = positions[None, :] <= query_places[:, None]
        scores = jnp.where(allowed[:, None, None, :], scores, -1e+30)
        weights = jnp.exp(scores - lax.optimization_barrier(jnp.max(scores, axis=-1, keepdims=True)))
        summed = jnp.einsum('sgrk,kgd->sgrd', weights, value_heads)
        return (summed / lax.optimization_barrier(jnp.sum(weights, axis=-1))[..., None]).astype(jnp.bfloat16)
    attended = lax.map(one_block, (grouped, starts)).reshape(sequence, H * HD)
    mixed_out = jnp.dot(attended, out_weight.T, preferred_element_type=jnp.float32)
    return mixed_out.astype(jnp.bfloat16)
```

```python
import math

import jax
import jax.numpy as jnp
from jax import lax
from jax.experimental import pallas as pl
from jax.experimental.pallas import tpu as pltpu
from jax.sharding import PartitionSpec as P

HD = 128
F32 = jnp.float32
BF16 = jnp.bfloat16
SCALE = math.log2(math.e) / math.sqrt(HD)
KEYS = 2048


def attention_kernel(q_ref, k_ref, v_ref, o_ref, acc, peak, total):
    rows = q_ref.shape[0]
    heads = q_ref.shape[1] // HD
    me = lax.axis_index("ctx")
    first = me * rows
    for h in range(heads):
        acc[h] = jnp.zeros((rows, HD), F32)
        peak[h] = jnp.full((rows, HD), -1e30, F32)
        total[h] = jnp.zeros((rows, HD), F32)

    def step(block, masked):
        at = pl.ds(pl.multiple_of(block * KEYS, KEYS), KEYS)
        k = k_ref[at, :]
        v = v_ref[at, :]
        v = jnp.concatenate([v, jnp.ones_like(v)], axis=1)
        if masked:
            row = lax.broadcasted_iota(jnp.int32, (rows, KEYS), 0) + first
            col = lax.broadcasted_iota(jnp.int32, (rows, KEYS), 1) + block * KEYS
            allowed = col <= row
        for h in range(heads):
            s = lax.dot_general(
                q_ref[:, h * HD : (h + 1) * HD], k, (((1,), (1,)), ((), ())), preferred_element_type=F32
            )
            if masked:
                s = jnp.where(allowed, s, -1e30)
            old = peak[h]
            new = jnp.maximum(old, jnp.max(s, axis=1, keepdims=True) * SCALE)
            alpha = jnp.exp2(old - new)
            p = jnp.exp2(s * SCALE - new[:, :1])
            pv = jnp.dot(p.astype(BF16), v, preferred_element_type=F32)
            acc[h] = acc[h] * alpha + pv[:, :HD]
            total[h] = total[h] * alpha + pv[:, HD:]
            peak[h] = new

    full = first // KEYS

    @pl.loop(0, full)
    def _(block):
        step(block, False)

    step(full, True)
    for h in range(heads):
        o_ref[:, h * HD : (h + 1) * HD] = (acc[h] / total[h]).astype(BF16)


def body(queries, keys, values, out_weight):
    rows, width = queries.shape
    heads = width // HD
    all_keys = lax.all_gather(keys, "ctx", axis=0, tiled=True)
    all_values = lax.all_gather(values, "ctx", axis=0, tiled=True)
    all_weight = lax.all_gather(out_weight, "ctx", axis=0, tiled=True)
    attended = pl.pallas_call(
        attention_kernel,
        out_shape=jax.ShapeDtypeStruct((rows, width), BF16),
        in_specs=[pl.BlockSpec(memory_space=pltpu.VMEM)] * 3,
        out_specs=pl.BlockSpec(memory_space=pltpu.VMEM),
        scratch_shapes=[pltpu.VMEM((heads, rows, HD), F32)] * 3,
        compiler_params=pltpu.CompilerParams(vmem_limit_bytes=48 * 2**20),
        cost_estimate=pl.CostEstimate(flops=4 * 10**9, bytes_accessed=5 * 2**20, transcendentals=0),
    )(queries, all_keys, all_values)
    partial_sums = lax.dot_general(
        attended, all_weight, (((1,), (1,)), ((), ())), preferred_element_type=F32
    ).astype(BF16)
    mixed_out = lax.psum_scatter(partial_sums, "tp", scatter_dimension=1, tiled=True)
    return mixed_out


def solution(mesh):
    return jax.shard_map(
        body,
        mesh=mesh,
        in_specs=(P("ctx", "tp"), P("ctx", "tp"), P("ctx", "tp"), P("ctx", "tp")),
        out_specs=P("ctx", "tp"),
        check_vma=False,
    )
```

```python
import math

import jax
import jax.numpy as jnp
from jax import lax
from jax.experimental import pallas as pl
from jax.experimental.pallas import tpu as pltpu
from jax.sharding import PartitionSpec as P

HD = 128
HEADS = 8
ROWS = 128
BOTH = 2 * ROWS
N = 4
TP = 8
WROWS = 64
F32 = jnp.float32
BF16 = jnp.bfloat16
SCALE = math.log2(math.e) / math.sqrt(HD)
NEG = -1e30
SUB = 2
SUBROWS = BOTH // SUB
KV, KVO, W, WO = range(4)
CROSS_K, CROSS_V, CROSS_W, SIB_Q, SIB_L, SIB_F = range(64, 70)
SIB_O = 70


def kernel(
    q_in, k_in, v_in, w_in, out,
    kbuf, vbuf, wbuf, qbuf, acc, peak, total, obuf, orecv, lbuf, lrecv, abuf,
    up_recv, dn_recv, up_send, dn_send, fin, fsend, frecv,
    ssem, rsem, usem_s, usem_r, dsem_s, dsem_r, lsem,
):
    me = lax.axis_index("ctx")
    tp = lax.axis_index("tp")
    zh = me // 32
    x = (me // 8) % N
    y = (me // 2) % N
    c = me % 2
    xn, xb = (x + 1) % N, (x + N - 1) % N
    yn, yb = (y + 1) % N, (y + N - 1) % N
    x2, y2 = (x + 2) % N, (y + 2) % N

    def at(z, i, j, k):
        return ((z * N + i) * N + j) * 2 + k

    xp, xm = at(zh, xn, y, c), at(zh, xb, y, c)
    yp, ym = at(zh, x, yn, c), at(zh, x, yb, c)
    zz, sib = at(1 - zh, x, y, c), at(zh, x, y, 1 - c)

    barrier = pltpu.get_barrier_semaphore()

    def greet(ctx, t):
        pl.semaphore_signal(barrier, inc=1, device_id=(ctx, t), device_id_type=pl.DeviceIdType.MESH)

    for dev in (xp, xm, yp, ym, zz, sib):
        greet(dev, tp)

    @pl.when(tp > 0)
    def _():
        greet(me, tp - 1)

    @pl.when(tp < TP - 1)
    def _():
        greet(me, tp + 1)

    loads = [
        pltpu.make_async_copy(k_in, kbuf.at[zh, x, y], lsem.at[0]),
        pltpu.make_async_copy(v_in, vbuf.at[zh, x, y], lsem.at[1]),
        pltpu.make_async_copy(w_in, wbuf.at[zh, x, y], lsem.at[2]),
        pltpu.make_async_copy(q_in, qbuf.at[c], lsem.at[3]),
    ]
    for load in loads:
        load.start()
    pl.semaphore_wait(barrier, 6 + (tp > 0).astype(jnp.int32) + (tp < TP - 1).astype(jnp.int32))

    def remote(src, dst, sem, ctx):
        return pltpu.make_async_remote_copy(
            src_ref=src, dst_ref=dst, send_sem=ssem.at[sem], recv_sem=rsem.at[sem],
            device_id=(ctx, tp), device_id_type=pl.DeviceIdType.MESH,
        )

    def got(dst, sem):
        remote(dst, dst, sem, sib).wait_recv()

    def views(inst):
        z = zh if inst in (KV, W) else 1 - zh
        if inst in (KV, KVO):
            return (kbuf, z, 0, ROWS), (vbuf, z, 0, ROWS)
        return (wbuf, z, 0, WROWS // 2), (wbuf, z, WROWS // 2, WROWS // 2)

    def block(view, i, j, part=None):
        buf, z, lo, n = view
        if part is not None:
            n = n // 2
            lo = lo + part * n
        return buf.at[z, i, j, pl.ds(lo, n)]

    everything = pl.ds(0, N)
    low, high = pl.ds(0, N // 2), pl.ds(N // 2, N // 2)

    def sends(inst, stage):
        a, b = views(inst)
        if stage == 0:
            return [
                (block(a, x, y), xp), (block(a, x, y), xm),
                (block(b, x, y), yp), (block(b, x, y), ym),
            ]
        if stage == 1:
            return [
                (block(a, xb, y, 0), xp), (block(a, xn, y, 1), xm),
                (block(b, x, yb, 0), yp), (block(b, x, yn, 1), ym),
            ]
        if stage == 2:
            return [
                (block(a, everything, y), yp), (block(a, everything, y), ym),
                (block(b, x, everything), xp), (block(b, x, everything), xm),
            ]
        return [
            (block(a, low, yb), yp), (block(a, high, yn), ym),
            (block(b, xb, low), xp), (block(b, xn, high), xm),
        ]

    def arrivals(inst, stage):
        a, b = views(inst)
        if stage == 0:
            return [block(a, xb, y), block(a, xn, y), block(b, x, yb), block(b, x, yn)]
        if stage == 1:
            return [block(a, x2, y, 0), block(a, x2, y, 1), block(b, x, y2, 0), block(b, x, y2, 1)]
        if stage == 2:
            return [
                block(a, everything, yb), block(a, everything, yn),
                block(b, xb, everything), block(b, xn, everything),
            ]
        return [block(a, low, y2), block(a, high, y2), block(b, x2, low), block(b, x2, high)]

    def event(inst, stage):
        base = inst * 16
        if stage > 0:
            for i, dst in enumerate(arrivals(inst, stage - 1)):
                got(dst, base + (stage - 1) * 4 + i)
        if stage < 4:
            for i, (ref, dev) in enumerate(sends(inst, stage)):
                remote(ref, ref, base + stage * 4 + i, dev).start()

    def drain(inst):
        for stage in range(4):
            for i, (ref, dev) in enumerate(sends(inst, stage)):
                remote(ref, ref, inst * 16 + stage * 4 + i, dev).wait_send()

    loads[0].wait()
    loads[1].wait()
    event(KV, 0)

    @pl.when(zh == 0)
    def _():
        remote(kbuf.at[zh, x, y], kbuf.at[zh, x, y], CROSS_K, zz).start()
        remote(vbuf.at[zh, x, y], vbuf.at[zh, x, y], CROSS_V, zz).start()

    loads[3].wait()
    remote(qbuf.at[c], qbuf.at[c], SIB_Q, sib).start()
    loads[2].wait()
    remote(wbuf.at[zh, x, y], wbuf.at[zh, x, y], CROSS_W, zz).start()
    event(W, 0)
    event(KV, 1)
    event(KV, 2)
    event(W, 1)
    event(KV, 3)
    event(W, 2)
    event(KV, 4)
    got(qbuf.at[1 - c], SIB_Q)

    @pl.when(zh == 1)
    def _():
        got(kbuf.at[1 - zh, x, y], CROSS_K)
        got(vbuf.at[1 - zh, x, y], CROSS_V)
        event(KVO, 0)

    keys = N * N * ROWS

    def scores(h, z):
        cols = pl.ds(pl.multiple_of(h * HD, HD), HD)
        q = qbuf[:, :, cols].reshape(BOTH, HD)
        k = kbuf[z].reshape(keys, HD)
        return lax.dot_general(q, k, (((1,), (1,)), ((), ())), preferred_element_type=F32)

    def weigh(s, z):
        m = jnp.max(s, axis=1, keepdims=True) * SCALE
        p = jnp.exp2(s * SCALE - m)
        v = vbuf[z].reshape(keys, HD)
        v = jnp.concatenate([v, jnp.ones_like(v)], axis=1)
        pv = jnp.dot(p.astype(BF16), v, preferred_element_type=F32)
        return jnp.broadcast_to(m, (BOTH, HD)), pv[:, :HD], pv[:, HD:]

    def finish(h):
        value = acc[h] / total[h]
        acc[h] = value
        obuf[h] = value.astype(BF16)
        lane = lax.broadcasted_iota(jnp.int32, (BOTH, HD), 1)
        lbuf[...] = jnp.where(lane == h, peak[h] + jnp.log2(total[h]), lbuf[...])
        oremote(h).start()

    def oremote(h):
        return pltpu.make_async_remote_copy(
            src_ref=obuf.at[h], dst_ref=orecv.at[h], send_sem=ssem.at[SIB_O + h], recv_sem=rsem.at[SIB_O + h],
            device_id=(sib, tp), device_id_type=pl.DeviceIdType.MESH,
        )

    def at_head(h, k, inst, stage):
        @pl.when(h == k)
        def _():
            event(inst, stage)

    lbuf[...] = jnp.zeros((BOTH, HD), F32)

    @pl.loop(0, HEADS)
    def _(h):
        s = scores(h, zh)
        row = lax.broadcasted_iota(jnp.int32, (BOTH, keys), 0) + (x * N + y) * BOTH
        col = lax.broadcasted_iota(jnp.int32, (BOTH, keys), 1)
        place = (col // ROWS) * BOTH + c * ROWS + col % ROWS
        s = jnp.where(place <= row, s, NEG)
        peak[h], acc[h], total[h] = weigh(s, zh)

        @pl.when(zh == 0)
        def _():
            finish(h)

        @pl.when(zh == 1)
        def _():
            at_head(h, 0, KVO, 1)
            at_head(h, 2, KVO, 2)
            at_head(h, 4, KVO, 3)

        at_head(h, 3, W, 3)
        at_head(h, 6, W, 4)

    got(wbuf.at[1 - zh, x, y], CROSS_W)
    event(WO, 0)

    @pl.when(zh == 0)
    def _():
        event(WO, 1)
        event(WO, 2)
        event(WO, 3)

    @pl.when(zh == 1)
    def _():
        event(KVO, 4)

        @pl.loop(0, HEADS)
        def _(h):
            m, pv, n = weigh(scores(h, 1 - zh), 1 - zh)
            old = peak[h]
            new = jnp.maximum(old, m)
            mine, theirs = jnp.exp2(old - new), jnp.exp2(m - new)
            acc[h] = acc[h] * mine + pv * theirs
            total[h] = total[h] * mine + n * theirs
            peak[h] = new
            finish(h)
            at_head(h, 0, WO, 1)
            at_head(h, 1, WO, 2)
            at_head(h, 5, WO, 3)

    lsend = pltpu.make_async_remote_copy(
        src_ref=lbuf, dst_ref=lrecv, send_sem=ssem.at[SIB_L], recv_sem=rsem.at[SIB_L],
        device_id=(sib, tp), device_id_type=pl.DeviceIdType.MESH,
    )
    lsend.start()
    lsend.wait_recv()
    for h in range(HEADS):
        oremote(h).wait_recv()
        share = 1.0 / (1.0 + jnp.exp2(lrecv[:, h : h + 1] - lbuf[:, h : h + 1]))
        other = orecv[h].astype(F32)
        abuf[:, h * HD : (h + 1) * HD] = (other + (acc[h] - other) * share).astype(BF16)

    event(WO, 4)

    def product(d):
        weight = wbuf[d // N, d % N].reshape(N * WROWS, HEADS * HD)
        return lax.dot_general(
            abuf[...], weight, (((1,), (1,)), ((), ())), preferred_element_type=F32
        )

    def hop(d, i, send, recv, s_sem, r_sem, to):
        rows = pl.ds(i * SUBROWS, SUBROWS)
        return pltpu.make_async_remote_copy(
            src_ref=send.at[d, rows], dst_ref=recv.at[d, rows],
            send_sem=s_sem.at[d, i], recv_sem=r_sem.at[d, i],
            device_id=(me, to), device_id_type=pl.DeviceIdType.MESH,
        )

    def up(d, i):
        return hop(d, i, up_send, up_recv, usem_s, usem_r, jnp.minimum(tp + 1, TP - 1))

    def down(d, i):
        return hop(d, i, dn_send, dn_recv, dsem_s, dsem_r, jnp.maximum(tp - 1, 0))

    @pl.loop(0, TP - 1)
    def _(k):
        d = TP - 1 - k

        @pl.when(tp < d)
        def _():
            fin[...] = product(d)
            for i in range(SUB):
                rows = slice(i * SUBROWS, (i + 1) * SUBROWS)

                @pl.when(tp > 0)
                def _():
                    up(d, i).wait_recv()
                    up_send[d, rows] = (fin[rows] + up_recv[d, rows].astype(F32)).astype(BF16)

                @pl.when(tp == 0)
                def _():
                    up_send[d, rows] = fin[rows].astype(BF16)

                up(d, i).start()

        @pl.when(tp > k)
        def _():
            fin[...] = product(k)
            for i in range(SUB):
                rows = slice(i * SUBROWS, (i + 1) * SUBROWS)

                @pl.when(tp < TP - 1)
                def _():
                    down(k, i).wait_recv()
                    dn_send[k, rows] = (fin[rows] + dn_recv[k, rows].astype(F32)).astype(BF16)

                @pl.when(tp == TP - 1)
                def _():
                    dn_send[k, rows] = fin[rows].astype(BF16)

                down(k, i).start()

    fin[...] = product(tp)

    @pl.when(tp > 0)
    def _():
        for i in range(SUB):
            up(tp, i).wait_recv()
        fin[...] += up_recv[tp].astype(F32)

    @pl.when(tp < TP - 1)
    def _():
        for i in range(SUB):
            down(tp, i).wait_recv()
        fin[...] += dn_recv[tp].astype(F32)

    def half(k):
        return fin[pl.ds(pl.multiple_of(k * ROWS, ROWS), ROWS), :].astype(BF16)

    fsend[...] = half(1 - c)
    frecv[c] = half(c)
    last = remote(fsend, frecv.at[c], SIB_F, sib)
    last.start()
    got(frecv.at[1 - c], SIB_F)
    for j in range(N):
        cols = slice(j * WROWS, (j + 1) * WROWS)
        out[:, j * 2 * WROWS : (j + 1) * 2 * WROWS] = jnp.concatenate(
            [frecv[0, :, cols], frecv[1, :, cols]], axis=1
        )

    last.wait_send()
    lsend.wait_send()
    for h in range(HEADS):
        oremote(h).wait_send()
    for inst in (KV, W, WO):
        drain(inst)

    @pl.when(zh == 1)
    def _():
        drain(KVO)

    @pl.when(zh == 0)
    def _():
        remote(kbuf.at[zh, x, y], kbuf.at[zh, x, y], CROSS_K, zz).wait_send()
        remote(vbuf.at[zh, x, y], vbuf.at[zh, x, y], CROSS_V, zz).wait_send()

    remote(wbuf.at[zh, x, y], wbuf.at[zh, x, y], CROSS_W, zz).wait_send()
    remote(qbuf.at[c], qbuf.at[c], SIB_Q, sib).wait_send()

    @pl.loop(0, TP - 1)
    def _(k):
        d = TP - 1 - k

        @pl.when(tp < d)
        def _():
            for i in range(SUB):
                up(d, i).wait_send()

        @pl.when(tp > k)
        def _():
            for i in range(SUB):
                down(k, i).wait_send()


def body(queries, keys, values, out_weight):
    slab = (2, N, N)
    sums = (TP, BOTH, BOTH)
    return pl.pallas_call(
        kernel,
        out_shape=jax.ShapeDtypeStruct((ROWS, TP * WROWS), BF16),
        in_specs=[pl.BlockSpec(memory_space=pl.ANY)] * 4,
        out_specs=pl.BlockSpec(memory_space=pltpu.VMEM),
        scratch_shapes=[
            pltpu.VMEM(slab + (ROWS, HD), BF16),
            pltpu.VMEM(slab + (ROWS, HD), BF16),
            pltpu.VMEM(slab + (WROWS, HEADS * HD), BF16),
            pltpu.VMEM((2, ROWS, HEADS * HD), BF16),
            pltpu.VMEM((HEADS, BOTH, HD), F32),
            pltpu.VMEM((HEADS, BOTH, HD), F32),
            pltpu.VMEM((HEADS, BOTH, HD), F32),
            pltpu.VMEM((HEADS, BOTH, HD), BF16),
            pltpu.VMEM((HEADS, BOTH, HD), BF16),
            pltpu.VMEM((BOTH, HD), F32),
            pltpu.VMEM((BOTH, HD), F32),
            pltpu.VMEM((BOTH, HEADS * HD), BF16),
            pltpu.VMEM(sums, BF16),
            pltpu.VMEM(sums, BF16),
            pltpu.VMEM(sums, BF16),
            pltpu.VMEM(sums, BF16),
            pltpu.VMEM((BOTH, BOTH), F32),
            pltpu.VMEM((ROWS, BOTH), BF16),
            pltpu.VMEM((2, ROWS, BOTH), BF16),
            pltpu.SemaphoreType.DMA((78,)),
            pltpu.SemaphoreType.DMA((78,)),
            pltpu.SemaphoreType.DMA((TP, SUB)),
            pltpu.SemaphoreType.DMA((TP, SUB)),
            pltpu.SemaphoreType.DMA((TP, SUB)),
            pltpu.SemaphoreType.DMA((TP, SUB)),
            pltpu.SemaphoreType.DMA((4,)),
        ],
        compiler_params=pltpu.CompilerParams(
            collective_id=0, has_side_effects=True, vmem_limit_bytes=56 * 2**20
        ),
        cost_estimate=pl.CostEstimate(flops=5 * 10**9, bytes_accessed=2**20, transcendentals=0),
    )(queries, keys, values, out_weight)


def solution(mesh):
    return jax.shard_map(
        body,
        mesh=mesh,
        in_specs=(P("ctx", "tp"), P("ctx", "tp"), P("ctx", "tp"), P("ctx", "tp")),
        out_specs=P("ctx", "tp"),
        check_vma=False,
    )
```

```python
import math

import jax
import jax.numpy as jnp
from jax import lax
from jax.experimental import pallas as pl
from jax.experimental.pallas import tpu as pltpu
from jax.sharding import PartitionSpec as P

HD = 128
HEADS = 8
ROWS = 128
BOTH = 2 * ROWS
N = 4
TP = 8
WROWS = 64
PIECE = WROWS // 2
F32 = jnp.float32
BF16 = jnp.bfloat16
SCALE = math.log2(math.e) / math.sqrt(HD)
NEG = -1e30
SUB = 4
HALF = SUB // 2
SUBROWS = BOTH // SUB
KV, KVO, WA, WB, OA, OB = range(6)
BEFORE = [(KV, 0), (WA, 0), (WB, 0), (KV, 1), (WA, 1), (KV, 2), (WB, 1), (KV, 3)]
FIRST_HALF = {0: [(OA, 0), (WA, 2)], 2: [(WB, 2)], 3: [(OA, 1)], 4: [(OB, 0)], 7: [(OB, 1)]}
FIRST_HALF_END = [(OA, 2), (OB, 2)]
LAST_HALF_BEGIN = [(KVO, 0)]
LAST_HALF = {0: [(WA, 2)], 2: [(KVO, 1)], 4: [(WB, 2)], 5: [(OA, 0)]}
LAST_HALF_MIDDLE = [(KVO, 2)]
LAST_HALF_MORE = {0: [(OB, 0), (OA, 1)], 3: [(OB, 1)], 4: [(OA, 2)], 6: [(OB, 2)]}
AFTER = [(WA, 3), (WB, 3), (OA, 3), (OB, 3)]
CROSS_K, CROSS_V, CROSS_W, SIB_Q, SIB_L, SIB_O, SIB_F = 96, 97, 98, 100, 101, 102, 110


def kernel(
    q_in, k_in, v_in, w_in, out,
    kbuf, vbuf, wbuf, qbuf, acc, peak, total, obuf, orecv, lbuf, lrecv, abuf,
    up_recv, dn_recv, up_send, dn_send, prod, fsend, frecv,
    ssem, rsem, usem_s, usem_r, dsem_s, dsem_r, lsem,
):
    me = lax.axis_index("ctx")
    tp = lax.axis_index("tp")
    zh = me // 32
    x = (me // 8) % N
    y = (me // 2) % N
    c = me % 2
    xn, xb = (x + 1) % N, (x + N - 1) % N
    yn, yb = (y + 1) % N, (y + N - 1) % N
    x2, y2 = (x + 2) % N, (y + 2) % N

    def at(z, i, j, k):
        return ((z * N + i) * N + j) * 2 + k

    xp, xm = at(zh, xn, y, c), at(zh, xb, y, c)
    yp, ym = at(zh, x, yn, c), at(zh, x, yb, c)
    xq, yq = at(zh, x2, y, c), at(zh, x, y2, c)
    zz, sib = at(1 - zh, x, y, c), at(zh, x, y, 1 - c)

    barrier = pltpu.get_barrier_semaphore()

    def greet(ctx, t):
        pl.semaphore_signal(barrier, inc=1, device_id=(ctx, t), device_id_type=pl.DeviceIdType.MESH)

    for dev in (xp, xm, xq, yp, ym, yq, zz, sib):
        greet(dev, tp)

    @pl.when(tp > 0)
    def _():
        greet(me, tp - 1)

    @pl.when(tp < TP - 1)
    def _():
        greet(me, tp + 1)

    loads = [
        pltpu.make_async_copy(k_in, kbuf.at[zh, x, y], lsem.at[0]),
        pltpu.make_async_copy(v_in, vbuf.at[zh, x, y], lsem.at[1]),
        pltpu.make_async_copy(w_in, wbuf.at[zh, x, y], lsem.at[2]),
        pltpu.make_async_copy(q_in, qbuf.at[c], lsem.at[3]),
    ]
    for load in loads:
        load.start()
    pl.semaphore_wait(barrier, 8 + (tp > 0).astype(jnp.int32) + (tp < TP - 1).astype(jnp.int32))

    def remote(src, dst, sem, ctx):
        return pltpu.make_async_remote_copy(
            src_ref=src, dst_ref=dst, send_sem=ssem.at[sem], recv_sem=rsem.at[sem],
            device_id=(ctx, tp), device_id_type=pl.DeviceIdType.MESH,
        )

    def got(dst, sem):
        remote(dst, dst, sem, sib).wait_recv()

    def views(inst):
        z = zh if inst in (KV, WA, WB) else 1 - zh
        if inst in (KV, KVO):
            return (kbuf, z, 0, ROWS), (vbuf, z, 0, ROWS)
        lo, n = (0 if inst in (WA, OA) else PIECE), PIECE // 2
        return (wbuf, z, lo, n), (wbuf, z, lo + n, n)

    def block(view, i, j):
        buf, z, lo, n = view
        return buf.at[z, i, j, pl.ds(lo, n)]

    everything = pl.ds(0, N)
    low, high = pl.ds(0, N // 2), pl.ds(N // 2, N // 2)

    def sends(inst, stage):
        a, b = views(inst)
        if stage == 0:
            return [(block(a, x, y), dev) for dev in (xp, xm, xq)] + [
                (block(b, x, y), dev) for dev in (yp, ym, yq)
            ]
        if inst == KVO and stage == 1:
            return [(block(a, everything, y), dev) for dev in (yp, ym, yq)] + [
                (block(b, x, everything), dev) for dev in (xp, xm, xq)
            ]
        if stage == 1:
            return [(block(a, everything, y), dev) for dev in (yp, ym)] + [
                (block(b, x, everything), dev) for dev in (xp, xm)
            ]
        if inst == KVO or stage == 3:
            return []
        return [
            (block(a, low, yb), yp), (block(a, high, yn), ym),
            (block(b, xb, low), xp), (block(b, xn, high), xm),
        ]

    def arrivals(inst, stage):
        a, b = views(inst)
        if stage == 0:
            return [block(a, i, y) for i in (xb, xn, x2)] + [block(b, x, j) for j in (yb, yn, y2)]
        if inst == KVO:
            return [block(a, everything, j) for j in (yb, yn, y2)] + [
                block(b, i, everything) for i in (xb, xn, x2)
            ]
        if stage == 1:
            return [block(a, everything, j) for j in (yb, yn)] + [
                block(b, i, everything) for i in (xb, xn)
            ]
        return [block(a, low, y2), block(a, high, y2), block(b, x2, low), block(b, x2, high)]

    def event(inst, stage):
        base = inst * 16
        if stage > 0:
            for i, dst in enumerate(arrivals(inst, stage - 1)):
                got(dst, base + (stage - 1) * 6 + i)
        elif inst == KVO:
            got(kbuf.at[1 - zh, x, y], CROSS_K)
            got(vbuf.at[1 - zh, x, y], CROSS_V)
        elif inst in (OA, OB):
            i = inst - OA
            got(wbuf.at[1 - zh, x, y, pl.ds(i * PIECE, PIECE)], CROSS_W + i)
        for i, (ref, dev) in enumerate(sends(inst, stage)):
            remote(ref, ref, base + stage * 6 + i, dev).start()

    def drain(inst):
        for stage in range(3):
            for i, (ref, dev) in enumerate(sends(inst, stage)):
                remote(ref, ref, inst * 16 + stage * 6 + i, dev).wait_send()

    def cross(i):
        ref = wbuf.at[zh, x, y, pl.ds(i * PIECE, PIECE)]
        return remote(ref, ref, CROSS_W + i, zz)

    loads[0].wait()
    loads[1].wait()

    @pl.when(zh == 0)
    def _():
        remote(kbuf.at[zh, x, y], kbuf.at[zh, x, y], CROSS_K, zz).start()
        remote(vbuf.at[zh, x, y], vbuf.at[zh, x, y], CROSS_V, zz).start()

    loads[2].wait()
    cross(0).start()
    cross(1).start()
    loads[3].wait()
    remote(qbuf.at[c], qbuf.at[c], SIB_Q, sib).start()
    for one in BEFORE:
        event(*one)
    got(qbuf.at[1 - c], SIB_Q)

    keys = N * N * ROWS

    def scores(h, z):
        cols = pl.ds(pl.multiple_of(h * HD, HD), HD)
        q = qbuf[:, :, cols].reshape(BOTH, HD)
        k = kbuf[z].reshape(keys, HD)
        return lax.dot_general(q, k, (((1,), (1,)), ((), ())), preferred_element_type=F32)

    def weigh(s, z):
        m = jnp.max(s, axis=1, keepdims=True) * SCALE
        p = jnp.exp2(s * SCALE - m)
        v = vbuf[z].reshape(keys, HD)
        v = jnp.concatenate([v, jnp.ones_like(v)], axis=1)
        pv = jnp.dot(p.astype(BF16), v, preferred_element_type=F32)
        return jnp.broadcast_to(m, (BOTH, HD)), pv[:, :HD], pv[:, HD:]

    def finish(h):
        value = acc[h] / total[h]
        acc[h] = value
        obuf[h] = value.astype(BF16)
        lane = lax.broadcasted_iota(jnp.int32, (BOTH, HD), 1)
        lbuf[...] = jnp.where(lane == h, peak[h] + jnp.log2(total[h]), lbuf[...])
        oremote(h).start()

    def oremote(h):
        return pltpu.make_async_remote_copy(
            src_ref=obuf.at[h], dst_ref=orecv.at[h], send_sem=ssem.at[SIB_O + h], recv_sem=rsem.at[SIB_O + h],
            device_id=(sib, tp), device_id_type=pl.DeviceIdType.MESH,
        )

    def at_head(h, table):
        for k, events in table.items():

            @pl.when(h == k)
            def _():
                for one in events:
                    event(*one)

    lbuf[...] = jnp.zeros((BOTH, HD), F32)

    @pl.when(zh == 1)
    def _():
        for one in LAST_HALF_BEGIN:
            event(*one)

    @pl.loop(0, HEADS)
    def _(h):
        s = scores(h, zh)
        row = lax.broadcasted_iota(jnp.int32, (BOTH, keys), 0) + (x * N + y) * BOTH
        col = lax.broadcasted_iota(jnp.int32, (BOTH, keys), 1)
        place = (col // ROWS) * BOTH + c * ROWS + col % ROWS
        s = jnp.where(place <= row, s, NEG)
        peak[h], acc[h], total[h] = weigh(s, zh)

        @pl.when(zh == 0)
        def _():
            finish(h)
            at_head(h, FIRST_HALF)

        @pl.when(zh == 1)
        def _():
            at_head(h, LAST_HALF)

    @pl.when(zh == 0)
    def _():
        for one in FIRST_HALF_END:
            event(*one)

    @pl.when(zh == 1)
    def _():
        for one in LAST_HALF_MIDDLE:
            event(*one)

        @pl.loop(0, HEADS)
        def _(h):
            m, pv, n = weigh(scores(h, 1 - zh), 1 - zh)
            old = peak[h]
            new = jnp.maximum(old, m)
            mine, theirs = jnp.exp2(old - new), jnp.exp2(m - new)
            acc[h] = acc[h] * mine + pv * theirs
            total[h] = total[h] * mine + n * theirs
            peak[h] = new
            finish(h)
            at_head(h, LAST_HALF_MORE)

    lsend = pltpu.make_async_remote_copy(
        src_ref=lbuf, dst_ref=lrecv, send_sem=ssem.at[SIB_L], recv_sem=rsem.at[SIB_L],
        device_id=(sib, tp), device_id_type=pl.DeviceIdType.MESH,
    )
    lsend.start()
    lsend.wait_recv()
    for h in range(HEADS):
        oremote(h).wait_recv()
        share = 1.0 / (1.0 + jnp.exp2(lrecv[:, h : h + 1] - lbuf[:, h : h + 1]))
        other = orecv[h].astype(F32)
        abuf[:, h * HD : (h + 1) * HD] = (other + (acc[h] - other) * share).astype(BF16)

    for one in AFTER:
        event(*one)

    def product(d):
        weight = wbuf[d // N, d % N].reshape(N * WROWS, HEADS * HD)
        return lax.dot_general(
            abuf[...], weight, (((1,), (1,)), ((), ())), preferred_element_type=F32
        )

    def sub(i):
        first = (1 - c) if i < HALF else c
        return pl.ds(pl.multiple_of(first * ROWS + (i % HALF) * SUBROWS, SUBROWS), SUBROWS)

    def hop(d, i, send, recv, s_sem, r_sem, to):
        rows = sub(i)
        return pltpu.make_async_remote_copy(
            src_ref=send.at[d, rows], dst_ref=recv.at[d, rows],
            send_sem=s_sem.at[d, i], recv_sem=r_sem.at[d, i],
            device_id=(me, to), device_id_type=pl.DeviceIdType.MESH,
        )

    def up(d, i):
        return hop(d, i, up_send, up_recv, usem_s, usem_r, jnp.minimum(tp + 1, TP - 1))

    def down(d, i):
        return hop(d, i, dn_send, dn_recv, dsem_s, dsem_r, jnp.maximum(tp - 1, 0))

    @pl.loop(0, TP - 1)
    def _(u):
        above = TP - 1 - u + tp
        below = u - TP + 1 + tp

        @pl.when(u >= tp)
        def _():
            prod[above] = product(above)

        @pl.when(below >= 0)
        def _():
            prod[below] = product(below)

        for i in range(SUB):
            rows = sub(i)

            @pl.when(u >= tp)
            def _():
                @pl.when(tp > 0)
                def _():
                    up(above, i).wait_recv()
                    up_send[above, rows] = (prod[above, rows] + up_recv[above, rows].astype(F32)).astype(BF16)

                @pl.when(tp == 0)
                def _():
                    up_send[above, rows] = prod[above, rows].astype(BF16)

                up(above, i).start()

            @pl.when(below >= 0)
            def _():
                @pl.when(tp < TP - 1)
                def _():
                    down(below, i).wait_recv()
                    dn_send[below, rows] = (prod[below, rows] + dn_recv[below, rows].astype(F32)).astype(BF16)

                @pl.when(tp == TP - 1)
                def _():
                    dn_send[below, rows] = prod[below, rows].astype(BF16)

                down(below, i).start()

    prod[tp] = product(tp)

    def last(i):
        rows = pl.ds((i % HALF) * SUBROWS, SUBROWS)
        return remote(fsend.at[rows], frecv.at[c, rows], SIB_F + i, sib)

    for i in range(SUB):
        rows = sub(i)

        @pl.when(tp > 0)
        def _():
            up(tp, i).wait_recv()
            prod[tp, rows] += up_recv[tp, rows].astype(F32)

        @pl.when(tp < TP - 1)
        def _():
            down(tp, i).wait_recv()
            prod[tp, rows] += dn_recv[tp, rows].astype(F32)

        part = pl.ds((i % HALF) * SUBROWS, SUBROWS)
        if i < HALF:
            fsend[part] = prod[tp, rows].astype(BF16)
            last(i).start()
        else:
            frecv[c, part] = prod[tp, rows].astype(BF16)
    for i in range(HALF):
        got(frecv.at[1 - c, pl.ds(i * SUBROWS, SUBROWS)], SIB_F + i)
    for j in range(N):
        cols = slice(j * WROWS, (j + 1) * WROWS)
        out[:, j * 2 * WROWS : (j + 1) * 2 * WROWS] = jnp.concatenate(
            [frecv[0, :, cols], frecv[1, :, cols]], axis=1
        )

    for i in range(HALF):
        last(i).wait_send()
    lsend.wait_send()
    for h in range(HEADS):
        oremote(h).wait_send()
    for inst in (KV, WA, WB, OA, OB):
        drain(inst)

    @pl.when(zh == 1)
    def _():
        drain(KVO)

    @pl.when(zh == 0)
    def _():
        remote(kbuf.at[zh, x, y], kbuf.at[zh, x, y], CROSS_K, zz).wait_send()
        remote(vbuf.at[zh, x, y], vbuf.at[zh, x, y], CROSS_V, zz).wait_send()

    cross(0).wait_send()
    cross(1).wait_send()
    remote(qbuf.at[c], qbuf.at[c], SIB_Q, sib).wait_send()

    @pl.loop(0, TP - 1)
    def _(k):
        d = TP - 1 - k

        @pl.when(tp < d)
        def _():
            for i in range(SUB):
                up(d, i).wait_send()

        @pl.when(tp > k)
        def _():
            for i in range(SUB):
                down(k, i).wait_send()


def body(queries, keys, values, out_weight):
    slab = (2, N, N)
    sums = (TP, BOTH, BOTH)
    return pl.pallas_call(
        kernel,
        out_shape=jax.ShapeDtypeStruct((ROWS, TP * WROWS), BF16),
        in_specs=[pl.BlockSpec(memory_space=pl.ANY)] * 4,
        out_specs=pl.BlockSpec(memory_space=pltpu.VMEM),
        scratch_shapes=[
            pltpu.VMEM(slab + (ROWS, HD), BF16),
            pltpu.VMEM(slab + (ROWS, HD), BF16),
            pltpu.VMEM(slab + (WROWS, HEADS * HD), BF16),
            pltpu.VMEM((2, ROWS, HEADS * HD), BF16),
            pltpu.VMEM((HEADS, BOTH, HD), F32),
            pltpu.VMEM((HEADS, BOTH, HD), F32),
            pltpu.VMEM((HEADS, BOTH, HD), F32),
            pltpu.VMEM((HEADS, BOTH, HD), BF16),
            pltpu.VMEM((HEADS, BOTH, HD), BF16),
            pltpu.VMEM((BOTH, HD), F32),
            pltpu.VMEM((BOTH, HD), F32),
            pltpu.VMEM((BOTH, HEADS * HD), BF16),
            pltpu.VMEM(sums, BF16),
            pltpu.VMEM(sums, BF16),
            pltpu.VMEM(sums, BF16),
            pltpu.VMEM(sums, BF16),
            pltpu.VMEM(sums, F32),
            pltpu.VMEM((ROWS, BOTH), BF16),
            pltpu.VMEM((2, ROWS, BOTH), BF16),
            pltpu.SemaphoreType.DMA((SIB_F + HALF,)),
            pltpu.SemaphoreType.DMA((SIB_F + HALF,)),
            pltpu.SemaphoreType.DMA((TP, SUB)),
            pltpu.SemaphoreType.DMA((TP, SUB)),
            pltpu.SemaphoreType.DMA((TP, SUB)),
            pltpu.SemaphoreType.DMA((TP, SUB)),
            pltpu.SemaphoreType.DMA((4,)),
        ],
        compiler_params=pltpu.CompilerParams(
            collective_id=0, has_side_effects=True, vmem_limit_bytes=56 * 2**20
        ),
        cost_estimate=pl.CostEstimate(flops=5 * 10**9, bytes_accessed=2**20, transcendentals=0),
    )(queries, keys, values, out_weight)


def solution(mesh):
    return jax.shard_map(
        body,
        mesh=mesh,
        in_specs=(P("ctx", "tp"), P("ctx", "tp"), P("ctx", "tp"), P("ctx", "tp")),
        out_specs=P("ctx", "tp"),
        check_vma=False,
    )
```

```python
import math

import jax
import jax.numpy as jnp
from jax import lax
from jax.experimental import pallas as pl
from jax.experimental.pallas import tpu as pltpu
from jax.sharding import PartitionSpec as P

HD = 128
HEADS = 8
ROWS = 128
BOTH = 2 * ROWS
N = 4
TP = 8
WROWS = 64
PIECE = WROWS // 2
F32 = jnp.float32
BF16 = jnp.bfloat16
SCALE = math.log2(math.e) / math.sqrt(HD)
NEG = -1e30
SUB = 2
SUBROWS = BOTH // SUB
PARTS = 2
COLS = BOTH // PARTS
KV, KVO, WA, WB, OA, OB = range(6)
BEFORE = [(WA, 0), (WB, 0), (KV, 1), (WA, 1)]
BEFORE_MORE = [(KV, 2), (WB, 1), (KV, 3)]
FIRST_HALF = {0: [(OA, 0), (WA, 2)], 2: [(WB, 2)], 3: [(OA, 1)], 4: [(OB, 0)], 7: [(OB, 1)]}
FIRST_HALF_END = []
LAST_HALF_BEGIN = [(KVO, 0)]
LAST_HALF = {0:[(WA,2)],1:[(WB,2)],2:[(KVO,1)],5:[(OA,0)],6:[(OB,0)]}
LAST_HALF_MIDDLE = [(OA,1),(KVO,2)]
LAST_HALF_MORE = {0:[(OB,1)],3:[(OA,2)],5:[(OB,2)]}
AFTER = [(WA, 3), (WB, 3)]
DURING = {1: [(OA, 2)], 2: [(OB, 2)]}
LAST = [(OA, 3), (OB, 3)]
CROSS_K, CROSS_V, CROSS_W, SIB_Q, SIB_L, SIB_O, SIB_F = 96, 97, 98, 100, 101, 102, 110


def kernel(
    q_in, k_in, v_in, w_in, out,
    kbuf, vbuf, wbuf, qbuf, acc, peak, total, obuf, orecv, lbuf, lrecv, abuf,
    up_recv, dn_recv, up_send, dn_send, prod, fsend, frecv,
    ssem, rsem, usem_s, usem_r, dsem_s, dsem_r, lsem,
):
    me = lax.axis_index("ctx")
    tp = lax.axis_index("tp")
    zh = me // 32
    x = (me // 8) % N
    y = (me // 2) % N
    c = me % 2
    xn, xb = (x + 1) % N, (x + N - 1) % N
    yn, yb = (y + 1) % N, (y + N - 1) % N
    x2, y2 = (x + 2) % N, (y + 2) % N

    def at(z, i, j, k):
        return ((z * N + i) * N + j) * 2 + k

    xp, xm = at(zh, xn, y, c), at(zh, xb, y, c)
    yp, ym = at(zh, x, yn, c), at(zh, x, yb, c)
    xq, yq = at(zh, x2, y, c), at(zh, x, y2, c)
    zz, sib = at(1 - zh, x, y, c), at(zh, x, y, 1 - c)

    barrier = pltpu.get_barrier_semaphore()

    def greet(ctx, t):
        pl.semaphore_signal(barrier, inc=1, device_id=(ctx, t), device_id_type=pl.DeviceIdType.MESH)

    for dev in (xp, xm, xq, yp, ym, yq, zz, sib):
        greet(dev, tp)

    @pl.when(tp > 0)
    def _():
        greet(me, tp - 1)

    @pl.when(tp < TP - 1)
    def _():
        greet(me, tp + 1)

    loads = [
        pltpu.make_async_copy(k_in, kbuf.at[zh, x, y], lsem.at[0]),
        pltpu.make_async_copy(v_in, vbuf.at[zh, x, y], lsem.at[1]),
        pltpu.make_async_copy(w_in, wbuf.at[zh, x, y], lsem.at[2]),
        pltpu.make_async_copy(q_in, qbuf.at[c], lsem.at[3]),
    ]
    for load in loads:
        load.start()
    pl.semaphore_wait(barrier, 8 + (tp > 0).astype(jnp.int32) + (tp < TP - 1).astype(jnp.int32))

    def remote(src, dst, sem, ctx):
        return pltpu.make_async_remote_copy(
            src_ref=src, dst_ref=dst, send_sem=ssem.at[sem], recv_sem=rsem.at[sem],
            device_id=(ctx, tp), device_id_type=pl.DeviceIdType.MESH,
        )

    def got(dst, sem):
        remote(dst, dst, sem, sib).wait_recv()

    def views(inst):
        z = zh if inst in (KV, WA, WB) else 1 - zh
        if inst in (KV, KVO):
            return (kbuf, z, 0, ROWS), (vbuf, z, 0, ROWS)
        lo, n = (0 if inst in (WA, OA) else PIECE), PIECE // 2
        return (wbuf, z, lo, n), (wbuf, z, lo + n, n)

    def block(view, i, j):
        buf, z, lo, n = view
        return buf.at[z, i, j, pl.ds(lo, n)]

    everything = pl.ds(0, N)
    low, high = pl.ds(0, N // 2), pl.ds(N // 2, N // 2)

    def sends(inst, stage):
        a, b = views(inst)
        if stage == 0:
            return [(block(a, x, y), dev) for dev in (xp, xm, xq)] + [
                (block(b, x, y), dev) for dev in (yp, ym, yq)
            ]
        if inst == KVO and stage == 1:
            return [(block(a, everything, y), dev) for dev in (yp, ym, yq)] + [
                (block(b, x, everything), dev) for dev in (xp, xm, xq)
            ]
        if stage == 1:
            return [(block(a, everything, y), dev) for dev in (yp, ym)] + [
                (block(b, x, everything), dev) for dev in (xp, xm)
            ]
        if inst == KVO or stage == 3:
            return []
        return [
            (block(a, low, yb), yp), (block(a, high, yn), ym),
            (block(b, xb, low), xp), (block(b, xn, high), xm),
        ]

    def arrivals(inst, stage):
        a, b = views(inst)
        if stage == 0:
            return [block(a, i, y) for i in (xb, xn, x2)] + [block(b, x, j) for j in (yb, yn, y2)]
        if inst == KVO:
            return [block(a, everything, j) for j in (yb, yn, y2)] + [
                block(b, i, everything) for i in (xb, xn, x2)
            ]
        if stage == 1:
            return [block(a, everything, j) for j in (yb, yn)] + [
                block(b, i, everything) for i in (xb, xn)
            ]
        return [block(a, low, y2), block(a, high, y2), block(b, x2, low), block(b, x2, high)]

    def event(inst, stage):
        base = inst * 16
        if stage > 0:
            for i, dst in enumerate(arrivals(inst, stage - 1)):
                got(dst, base + (stage - 1) * 6 + i)
        elif inst == KVO:
            got(kbuf.at[1 - zh, x, y], CROSS_K)
            got(vbuf.at[1 - zh, x, y], CROSS_V)
        elif inst in (OA, OB):
            i = inst - OA
            got(wbuf.at[1 - zh, x, y, pl.ds(i * PIECE, PIECE)], CROSS_W + i)
        for i, (ref, dev) in enumerate(sends(inst, stage)):
            remote(ref, ref, base + stage * 6 + i, dev).start()

    def drain(inst):
        for stage in range(3):
            for i, (ref, dev) in enumerate(sends(inst, stage)):
                remote(ref, ref, inst * 16 + stage * 6 + i, dev).wait_send()

    def cross(i):
        ref = wbuf.at[zh, x, y, pl.ds(i * PIECE, PIECE)]
        return remote(ref, ref, CROSS_W + i, zz)

    loads[0].wait()
    loads[1].wait()

    @pl.when(zh == 0)
    def _():
        remote(kbuf.at[zh, x, y], kbuf.at[zh, x, y], CROSS_K, zz).start()
        remote(vbuf.at[zh, x, y], vbuf.at[zh, x, y], CROSS_V, zz).start()

    event(KV, 0)
    loads[2].wait()

    @pl.when(zh == 0)
    def _():
        cross(0).start()
        cross(1).start()

    loads[3].wait()
    remote(qbuf.at[c], qbuf.at[c], SIB_Q, sib).start()
    for one in BEFORE:
        event(*one)

    @pl.when(zh == 1)
    def _():
        cross(0).start()
        cross(1).start()

    for one in BEFORE_MORE:
        event(*one)
    got(qbuf.at[1 - c], SIB_Q)

    keys = N * N * ROWS

    def scores(h, z):
        cols = pl.ds(pl.multiple_of(h * HD, HD), HD)
        q = qbuf[:, :, cols].reshape(BOTH, HD)
        k = kbuf[z].reshape(keys, HD)
        return lax.dot_general(q, k, (((1,), (1,)), ((), ())), preferred_element_type=F32)

    def weigh(s, z):
        m = jnp.max(s, axis=1, keepdims=True) * SCALE
        p = jnp.exp2(s * SCALE - m)
        v = vbuf[z].reshape(keys, HD)
        v = jnp.concatenate([v, jnp.ones_like(v)], axis=1)
        pv = jnp.dot(p.astype(BF16), v, preferred_element_type=F32)
        return jnp.broadcast_to(m, (BOTH, HD)), pv[:, :HD], pv[:, HD:]

    def finish(h):
        value = acc[h] / total[h]
        acc[h] = value
        obuf[h] = value.astype(BF16)
        lane = lax.broadcasted_iota(jnp.int32, (BOTH, HD), 1)
        lbuf[...] = jnp.where(lane == h, peak[h] + jnp.log2(total[h]), lbuf[...])
        oremote(h).start()

    def oremote(h):
        return pltpu.make_async_remote_copy(
            src_ref=obuf.at[h], dst_ref=orecv.at[h], send_sem=ssem.at[SIB_O + h], recv_sem=rsem.at[SIB_O + h],
            device_id=(sib, tp), device_id_type=pl.DeviceIdType.MESH,
        )

    def at_head(h, table):
        for k, events in table.items():

            @pl.when(h == k)
            def _():
                for one in events:
                    event(*one)

    lbuf[...] = jnp.zeros((BOTH, HD), F32)

    @pl.when(zh == 1)
    def _():
        for one in LAST_HALF_BEGIN:
            event(*one)

    @pl.loop(0, HEADS)
    def _(h):
        s = scores(h, zh)
        row = lax.broadcasted_iota(jnp.int32, (BOTH, keys), 0) + (x * N + y) * BOTH
        col = lax.broadcasted_iota(jnp.int32, (BOTH, keys), 1)
        place = (col // ROWS) * BOTH + c * ROWS + col % ROWS
        s = jnp.where(place <= row, s, NEG)
        peak[h], acc[h], total[h] = weigh(s, zh)

        @pl.when(zh == 0)
        def _():
            finish(h)
            at_head(h, FIRST_HALF)

        @pl.when(zh == 1)
        def _():
            at_head(h, LAST_HALF)

    @pl.when(zh == 0)
    def _():
        for one in FIRST_HALF_END:
            event(*one)

    @pl.when(zh == 1)
    def _():
        for one in LAST_HALF_MIDDLE:
            event(*one)

        @pl.loop(0, HEADS)
        def _(h):
            m, pv, n = weigh(scores(h, 1 - zh), 1 - zh)
            old = peak[h]
            new = jnp.maximum(old, m)
            mine, theirs = jnp.exp2(old - new), jnp.exp2(m - new)
            acc[h] = acc[h] * mine + pv * theirs
            total[h] = total[h] * mine + n * theirs
            peak[h] = new
            finish(h)
            at_head(h, LAST_HALF_MORE)

    lsend = pltpu.make_async_remote_copy(
        src_ref=lbuf, dst_ref=lrecv, send_sem=ssem.at[SIB_L], recv_sem=rsem.at[SIB_L],
        device_id=(sib, tp), device_id_type=pl.DeviceIdType.MESH,
    )
    lsend.start()
    lsend.wait_recv()
    for h in range(HEADS):
        oremote(h).wait_recv()
        share = 1.0 / (1.0 + jnp.exp2(lrecv[:, h : h + 1] - lbuf[:, h : h + 1]))
        other = orecv[h].astype(F32)
        abuf[:, h * HD : (h + 1) * HD] = (other + (acc[h] - other) * share).astype(BF16)


    def product(p, d):
        weight = wbuf[d // N, d % N, :, p * PIECE : (p + 1) * PIECE, :].reshape(COLS, HEADS * HD)
        return lax.dot_general(
            abuf[...], weight, (((1,), (1,)), ((), ())), preferred_element_type=F32
        )

    def sub(i):
        first = (1 - c) if i == 0 else c
        return pl.ds(pl.multiple_of(first * ROWS, ROWS), ROWS)

    def hop(p, d, i, send, recv, s_sem, r_sem, to):
        rows = sub(i)
        return pltpu.make_async_remote_copy(
            src_ref=send.at[p, d, rows], dst_ref=recv.at[p, d, rows],
            send_sem=s_sem.at[p, d, i], recv_sem=r_sem.at[p, d, i],
            device_id=(me, to), device_id_type=pl.DeviceIdType.MESH,
        )

    def up(p, d, i):
        return hop(p, d, i, up_send, up_recv, usem_s, usem_r, jnp.minimum(tp + 1, TP - 1))

    def down(p, d, i):
        return hop(p, d, i, dn_send, dn_recv, dsem_s, dsem_r, jnp.maximum(tp - 1, 0))

    def chain(p, step):
        nth_up = step - tp
        nth_down = step - (TP - 1) + tp
        above = TP - 1 - nth_up
        above = jnp.where(zh == 0, jnp.where(nth_up < N - 1, above - N, above + N - 1), above)
        below = nth_down
        rises = (nth_up >= 0) & (nth_up < TP - 1) & (above > tp)
        falls = (nth_down >= 0) & (nth_down < TP - 1) & (below < tp)
        above = jnp.clip(above, 0, TP - 1)
        below = jnp.clip(below, 0, TP - 1)

        @pl.when(rises)
        def _():
            prod[p, above] = product(p, above)

        @pl.when(falls)
        def _():
            prod[p, below] = product(p, below)

        for i in range(SUB):
            rows = sub(i)

            @pl.when(rises)
            def _():
                @pl.when(tp > 0)
                def _():
                    up(p, above, i).wait_recv()
                    up_send[p, above, rows] = (prod[p, above, rows] + up_recv[p, above, rows].astype(F32)).astype(BF16)

                @pl.when(tp == 0)
                def _():
                    up_send[p, above, rows] = prod[p, above, rows].astype(BF16)

                up(p, above, i).start()

            @pl.when(falls)
            def _():
                @pl.when(tp < TP - 1)
                def _():
                    down(p, below, i).wait_recv()
                    dn_send[p, below, rows] = (prod[p, below, rows] + dn_recv[p, below, rows].astype(F32)).astype(BF16)

                @pl.when(tp == TP - 1)
                def _():
                    dn_send[p, below, rows] = prod[p, below, rows].astype(BF16)

                down(p, below, i).start()

    for one in AFTER:
        event(*one)

    @pl.loop(0, TP + 2)
    def _(step):
        for k, events in DURING.items():

            @pl.when((step == k) & (zh == 0))
            def _():
                for one in events:
                    event(*one)

        @pl.when(step == jnp.where(zh == 0, N - 1, jnp.minimum(TP - 1 - tp, tp + N)))
        def _():
            for one in LAST:
                event(*one)

        for p in range(PARTS):
            chain(p, step)

    for p in range(PARTS):
        prod[p, tp] = product(p, tp)
    for inst in (KV, WA, WB, OA, OB):
        drain(inst)

    def last(p):
        return remote(fsend.at[p], frecv.at[c, p], SIB_F + p, sib)

    for p in range(PARTS):
        for i in range(SUB):
            rows = sub(i)

            @pl.when(tp > 0)
            def _():
                up(p, tp, i).wait_recv()
                prod[p, tp, rows] += up_recv[p, tp, rows].astype(F32)

            @pl.when(tp < TP - 1)
            def _():
                down(p, tp, i).wait_recv()
                prod[p, tp, rows] += dn_recv[p, tp, rows].astype(F32)

            if i == 0:
                fsend[p] = prod[p, tp, rows].astype(BF16)
                last(p).start()
            else:
                frecv[c, p] = prod[p, tp, rows].astype(BF16)
    for p in range(PARTS):
        got(frecv.at[1 - c, p], SIB_F + p)
    for j in range(N):
        cols = slice(j * PIECE, (j + 1) * PIECE)
        out[:, j * 2 * WROWS : (j + 1) * 2 * WROWS] = jnp.concatenate(
            [frecv[k, p, :, cols] for k in range(2) for p in range(PARTS)], axis=1
        )

    for p in range(PARTS):
        last(p).wait_send()
    lsend.wait_send()
    for h in range(HEADS):
        oremote(h).wait_send()
    @pl.when(zh == 1)
    def _():
        drain(KVO)

    @pl.when(zh == 0)
    def _():
        remote(kbuf.at[zh, x, y], kbuf.at[zh, x, y], CROSS_K, zz).wait_send()
        remote(vbuf.at[zh, x, y], vbuf.at[zh, x, y], CROSS_V, zz).wait_send()

    cross(0).wait_send()
    cross(1).wait_send()
    remote(qbuf.at[c], qbuf.at[c], SIB_Q, sib).wait_send()

    @pl.loop(0, TP - 1)
    def _(k):
        d = TP - 1 - k

        @pl.when(tp < d)
        def _():
            for p in range(PARTS):
                for i in range(SUB):
                    up(p, d, i).wait_send()

        @pl.when(tp > k)
        def _():
            for p in range(PARTS):
                for i in range(SUB):
                    down(p, k, i).wait_send()


def body(queries, keys, values, out_weight):
    slab = (2, N, N)
    sums = (PARTS, TP, BOTH, COLS)
    return pl.pallas_call(
        kernel,
        out_shape=jax.ShapeDtypeStruct((ROWS, TP * WROWS), BF16),
        in_specs=[pl.BlockSpec(memory_space=pl.ANY)] * 4,
        out_specs=pl.BlockSpec(memory_space=pltpu.VMEM),
        scratch_shapes=[
            pltpu.VMEM(slab + (ROWS, HD), BF16),
            pltpu.VMEM(slab + (ROWS, HD), BF16),
            pltpu.VMEM(slab + (WROWS, HEADS * HD), BF16),
            pltpu.VMEM((2, ROWS, HEADS * HD), BF16),
            pltpu.VMEM((HEADS, BOTH, HD), F32),
            pltpu.VMEM((HEADS, BOTH, HD), F32),
            pltpu.VMEM((HEADS, BOTH, HD), F32),
            pltpu.VMEM((HEADS, BOTH, HD), BF16),
            pltpu.VMEM((HEADS, BOTH, HD), BF16),
            pltpu.VMEM((BOTH, HD), F32),
            pltpu.VMEM((BOTH, HD), F32),
            pltpu.VMEM((BOTH, HEADS * HD), BF16),
            pltpu.VMEM(sums, BF16),
            pltpu.VMEM(sums, BF16),
            pltpu.VMEM(sums, BF16),
            pltpu.VMEM(sums, BF16),
            pltpu.VMEM(sums, F32),
            pltpu.VMEM((PARTS, ROWS, COLS), BF16),
            pltpu.VMEM((2, PARTS, ROWS, COLS), BF16),
            pltpu.SemaphoreType.DMA((SIB_F + PARTS,)),
            pltpu.SemaphoreType.DMA((SIB_F + PARTS,)),
            pltpu.SemaphoreType.DMA((PARTS, TP, SUB)),
            pltpu.SemaphoreType.DMA((PARTS, TP, SUB)),
            pltpu.SemaphoreType.DMA((PARTS, TP, SUB)),
            pltpu.SemaphoreType.DMA((PARTS, TP, SUB)),
            pltpu.SemaphoreType.DMA((4,)),
        ],
        compiler_params=pltpu.CompilerParams(
            collective_id=0, has_side_effects=True, vmem_limit_bytes=56 * 2**20
        ),
        cost_estimate=pl.CostEstimate(flops=5 * 10**9, bytes_accessed=2**20, transcendentals=0),
    )(queries, keys, values, out_weight)


def solution(mesh):
    return jax.shard_map(
        body,
        mesh=mesh,
        in_specs=(P("ctx", "tp"), P("ctx", "tp"), P("ctx", "tp"), P("ctx", "tp")),
        out_specs=P("ctx", "tp"),
        check_vma=False,
    )
```

```python
import math

import jax
import jax.numpy as jnp
from jax import lax
from jax.experimental import pallas as pl
from jax.experimental.pallas import tpu as pltpu
from jax.sharding import PartitionSpec as P

HD = 128
HEADS = 8
ROWS = 128
BOTH = 2 * ROWS
N = 4
TP = 8
WROWS = 64
PIECE = WROWS // 2
F32 = jnp.float32
BF16 = jnp.bfloat16
SCALE = math.log2(math.e) / math.sqrt(HD)
NEG = -1e30
SUB = 2
SUBROWS = BOTH // SUB
PARTS = 2
COLS = BOTH // PARTS
KV, KVO, WA, WB, OA, OB = range(6)
BEFORE = [(WA, 0), (WB, 0), (KV, 1), (WA, 1)]
BEFORE_MORE = [(KV, 2), (WB, 1), (KV, 3)]
FIRST_HALF = {0: [(OA, 0), (WA, 2)], 2: [(WB, 2)], 3: [(OA, 1)], 4: [(OB, 0)], 7: [(OB, 1)]}
FIRST_HALF_END = []
LAST_HALF_BEGIN = [(KVO, 0)]
LAST_HALF = {0:[(WA,2)],1:[(WB,2)],2:[(KVO,1)],5:[(OA,0)],6:[(OB,0)]}
LAST_HALF_MIDDLE = [(OA,1),(KVO,2)]
LAST_HALF_MORE = {0:[(OB,1)],3:[(OA,2)],5:[(OB,2)]}
AFTER = [(WA, 3), (WB, 3)]
DURING = {1: [(OA, 2)], 2: [(OB, 2)]}
LAST = [(OA, 3)], [(OB, 3)]
CROSS_K, CROSS_V, CROSS_W, SIB_Q, SIB_L, SIB_O, SIB_F = 96, 97, 98, 100, 101, 102, 110


def kernel(
    q_in, k_in, v_in, w_in, out,
    kbuf, vbuf, wbuf, qbuf, acc, peak, total, obuf, orecv, lbuf, lrecv, abuf,
    up_recv, dn_recv, up_send, dn_send, prod, fsend, frecv,
    ssem, rsem, usem_s, usem_r, dsem_s, dsem_r, lsem,
):
    me = lax.axis_index("ctx")
    tp = lax.axis_index("tp")
    zh = me // 32
    x = (me // 8) % N
    y = (me // 2) % N
    c = me % 2
    xn, xb = (x + 1) % N, (x + N - 1) % N
    yn, yb = (y + 1) % N, (y + N - 1) % N
    x2, y2 = (x + 2) % N, (y + 2) % N

    def at(z, i, j, k):
        return ((z * N + i) * N + j) * 2 + k

    xp, xm = at(zh, xn, y, c), at(zh, xb, y, c)
    yp, ym = at(zh, x, yn, c), at(zh, x, yb, c)
    xq, yq = at(zh, x2, y, c), at(zh, x, y2, c)
    zz, sib = at(1 - zh, x, y, c), at(zh, x, y, 1 - c)

    barrier = pltpu.get_barrier_semaphore()

    def greet(ctx, t):
        pl.semaphore_signal(barrier, inc=1, device_id=(ctx, t), device_id_type=pl.DeviceIdType.MESH)

    for dev in (xp, xm, xq, yp, ym, yq, zz, sib):
        greet(dev, tp)

    @pl.when(tp > 0)
    def _():
        greet(me, tp - 1)

    @pl.when(tp < TP - 1)
    def _():
        greet(me, tp + 1)

    loads = [
        pltpu.make_async_copy(k_in, kbuf.at[zh, x, y], lsem.at[0]),
        pltpu.make_async_copy(v_in, vbuf.at[zh, x, y], lsem.at[1]),
        pltpu.make_async_copy(w_in, wbuf.at[zh, x, y], lsem.at[2]),
        pltpu.make_async_copy(q_in, qbuf.at[c], lsem.at[3]),
    ]
    for load in loads:
        load.start()
    pl.semaphore_wait(barrier, 8 + (tp > 0).astype(jnp.int32) + (tp < TP - 1).astype(jnp.int32))

    def remote(src, dst, sem, ctx):
        return pltpu.make_async_remote_copy(
            src_ref=src, dst_ref=dst, send_sem=ssem.at[sem], recv_sem=rsem.at[sem],
            device_id=(ctx, tp), device_id_type=pl.DeviceIdType.MESH,
        )

    def got(dst, sem):
        remote(dst, dst, sem, sib).wait_recv()

    def views(inst):
        z = zh if inst in (KV, WA, WB) else 1 - zh
        if inst in (KV, KVO):
            return (kbuf, z, 0, ROWS), (vbuf, z, 0, ROWS)
        lo, n = (0 if inst in (WA, OA) else PIECE), PIECE // 2
        return (wbuf, z, lo, n), (wbuf, z, lo + n, n)

    def block(view, i, j):
        buf, z, lo, n = view
        return buf.at[z, i, j, pl.ds(lo, n)]

    everything = pl.ds(0, N)
    low, high = pl.ds(0, N // 2), pl.ds(N // 2, N // 2)

    def sends(inst, stage):
        a, b = views(inst)
        if stage == 0:
            return [(block(a, x, y), dev) for dev in (xp, xm, xq)] + [
                (block(b, x, y), dev) for dev in (yp, ym, yq)
            ]
        if inst == KVO and stage == 1:
            return [(block(a, everything, y), dev) for dev in (yp, ym, yq)] + [
                (block(b, x, everything), dev) for dev in (xp, xm, xq)
            ]
        if stage == 1:
            return [(block(a, everything, y), dev) for dev in (yp, ym)] + [
                (block(b, x, everything), dev) for dev in (xp, xm)
            ]
        if inst == KVO or stage == 3:
            return []
        return [
            (block(a, low, yb), yp), (block(a, high, yn), ym),
            (block(b, xb, low), xp), (block(b, xn, high), xm),
        ]

    def arrivals(inst, stage):
        a, b = views(inst)
        if stage == 0:
            return [block(a, i, y) for i in (xb, xn, x2)] + [block(b, x, j) for j in (yb, yn, y2)]
        if inst == KVO:
            return [block(a, everything, j) for j in (yb, yn, y2)] + [
                block(b, i, everything) for i in (xb, xn, x2)
            ]
        if stage == 1:
            return [block(a, everything, j) for j in (yb, yn)] + [
                block(b, i, everything) for i in (xb, xn)
            ]
        return [block(a, low, y2), block(a, high, y2), block(b, x2, low), block(b, x2, high)]

    def event(inst, stage):
        base = inst * 16
        if stage > 0:
            for i, dst in enumerate(arrivals(inst, stage - 1)):
                got(dst, base + (stage - 1) * 6 + i)
        elif inst == KVO:
            got(kbuf.at[1 - zh, x, y], CROSS_K)
            got(vbuf.at[1 - zh, x, y], CROSS_V)
        elif inst in (OA, OB):
            i = inst - OA
            got(wbuf.at[1 - zh, x, y, pl.ds(i * PIECE, PIECE)], CROSS_W + i)
        for i, (ref, dev) in enumerate(sends(inst, stage)):
            remote(ref, ref, base + stage * 6 + i, dev).start()

    def drain(inst):
        for stage in range(3):
            for i, (ref, dev) in enumerate(sends(inst, stage)):
                remote(ref, ref, inst * 16 + stage * 6 + i, dev).wait_send()

    def cross(i):
        ref = wbuf.at[zh, x, y, pl.ds(i * PIECE, PIECE)]
        return remote(ref, ref, CROSS_W + i, zz)

    loads[0].wait()
    loads[1].wait()

    @pl.when(zh == 0)
    def _():
        remote(kbuf.at[zh, x, y], kbuf.at[zh, x, y], CROSS_K, zz).start()
        remote(vbuf.at[zh, x, y], vbuf.at[zh, x, y], CROSS_V, zz).start()

    event(KV, 0)
    loads[2].wait()

    @pl.when(zh == 0)
    def _():
        cross(0).start()
        cross(1).start()

    loads[3].wait()
    remote(qbuf.at[c], qbuf.at[c], SIB_Q, sib).start()
    for one in BEFORE:
        event(*one)

    @pl.when(zh == 1)
    def _():
        cross(0).start()
        cross(1).start()

    for one in BEFORE_MORE:
        event(*one)
    got(qbuf.at[1 - c], SIB_Q)

    keys = N * N * ROWS

    def scores(h, z):
        cols = pl.ds(pl.multiple_of(h * HD, HD), HD)
        q = qbuf[:, :, cols].reshape(BOTH, HD)
        k = kbuf[z].reshape(keys, HD)
        return lax.dot_general(q, k, (((1,), (1,)), ((), ())), preferred_element_type=F32)

    def weigh(s, z):
        m = jnp.max(s, axis=1, keepdims=True) * SCALE
        p = jnp.exp2(s * SCALE - m)
        v = vbuf[z].reshape(keys, HD)
        v = jnp.concatenate([v, jnp.ones_like(v)], axis=1)
        pv = jnp.dot(p.astype(BF16), v, preferred_element_type=F32)
        return jnp.broadcast_to(m, (BOTH, HD)), pv[:, :HD], pv[:, HD:]

    def finish(h):
        value = acc[h] / total[h]
        acc[h] = value
        obuf[h] = value.astype(BF16)
        lane = lax.broadcasted_iota(jnp.int32, (BOTH, HD), 1)
        lbuf[...] = jnp.where(lane == h, peak[h] + jnp.log2(total[h]), lbuf[...])
        oremote(h).start()

    def oremote(h):
        return pltpu.make_async_remote_copy(
            src_ref=obuf.at[h], dst_ref=orecv.at[h], send_sem=ssem.at[SIB_O + h], recv_sem=rsem.at[SIB_O + h],
            device_id=(sib, tp), device_id_type=pl.DeviceIdType.MESH,
        )

    def at_head(h, table):
        for k, events in table.items():

            @pl.when(h == k)
            def _():
                for one in events:
                    event(*one)

    lbuf[...] = jnp.zeros((BOTH, HD), F32)

    @pl.when(zh == 1)
    def _():
        for one in LAST_HALF_BEGIN:
            event(*one)

    @pl.loop(0, HEADS)
    def _(h):
        s = scores(h, zh)
        row = lax.broadcasted_iota(jnp.int32, (BOTH, keys), 0) + (x * N + y) * BOTH
        col = lax.broadcasted_iota(jnp.int32, (BOTH, keys), 1)
        place = (col // ROWS) * BOTH + c * ROWS + col % ROWS
        s = jnp.where(place <= row, s, NEG)
        peak[h], acc[h], total[h] = weigh(s, zh)

        @pl.when(zh == 0)
        def _():
            finish(h)
            at_head(h, FIRST_HALF)

        @pl.when(zh == 1)
        def _():
            at_head(h, LAST_HALF)

    @pl.when(zh == 0)
    def _():
        for one in FIRST_HALF_END:
            event(*one)

    @pl.when(zh == 1)
    def _():
        for one in LAST_HALF_MIDDLE:
            event(*one)

        @pl.loop(0, HEADS)
        def _(h):
            m, pv, n = weigh(scores(h, 1 - zh), 1 - zh)
            old = peak[h]
            new = jnp.maximum(old, m)
            mine, theirs = jnp.exp2(old - new), jnp.exp2(m - new)
            acc[h] = acc[h] * mine + pv * theirs
            total[h] = total[h] * mine + n * theirs
            peak[h] = new
            finish(h)
            at_head(h, LAST_HALF_MORE)

    lsend = pltpu.make_async_remote_copy(
        src_ref=lbuf, dst_ref=lrecv, send_sem=ssem.at[SIB_L], recv_sem=rsem.at[SIB_L],
        device_id=(sib, tp), device_id_type=pl.DeviceIdType.MESH,
    )
    lsend.start()
    lsend.wait_recv()
    for h in range(HEADS):
        oremote(h).wait_recv()
        share = 1.0 / (1.0 + jnp.exp2(lrecv[:, h : h + 1] - lbuf[:, h : h + 1]))
        other = orecv[h].astype(F32)
        abuf[:, h * HD : (h + 1) * HD] = (other + (acc[h] - other) * share).astype(BF16)


    def product(p, d):
        weight = wbuf[d // N, d % N, :, p * PIECE : (p + 1) * PIECE, :].reshape(COLS, HEADS * HD)
        return lax.dot_general(
            abuf[...], weight, (((1,), (1,)), ((), ())), preferred_element_type=F32
        )

    def sub(i):
        first = (1 - c) if i == 0 else c
        return pl.ds(pl.multiple_of(first * ROWS, ROWS), ROWS)

    def hop(p, d, i, send, recv, s_sem, r_sem, to):
        rows = sub(i)
        return pltpu.make_async_remote_copy(
            src_ref=send.at[p, d, rows], dst_ref=recv.at[p, d, rows],
            send_sem=s_sem.at[p, d, i], recv_sem=r_sem.at[p, d, i],
            device_id=(me, to), device_id_type=pl.DeviceIdType.MESH,
        )

    def up(p, d, i):
        return hop(p, d, i, up_send, up_recv, usem_s, usem_r, jnp.minimum(tp + 1, TP - 1))

    def down(p, d, i):
        return hop(p, d, i, dn_send, dn_recv, dsem_s, dsem_r, jnp.maximum(tp - 1, 0))

    def chain(p, step):
        nth_up = step - tp
        nth_down = step - (TP - 1) + tp
        above = TP - 1 - nth_up
        above = jnp.where(zh == 0, jnp.where(nth_up < N - 1, above - N, above + N - 1), above)
        below = nth_down
        rises = (nth_up >= 0) & (nth_up < TP - 1) & (above > tp)
        falls = (nth_down >= 0) & (nth_down < TP - 1) & (below < tp)
        above = jnp.clip(above, 0, TP - 1)
        below = jnp.clip(below, 0, TP - 1)

        @pl.when(rises)
        def _():
            prod[p, above] = product(p, above)

        @pl.when(falls)
        def _():
            prod[p, below] = product(p, below)

        for i in range(SUB):
            rows = sub(i)

            @pl.when(rises)
            def _():
                @pl.when(tp > 0)
                def _():
                    up(p, above, i).wait_recv()
                    up_send[p, above, rows] = (prod[p, above, rows] + up_recv[p, above, rows].astype(F32)).astype(BF16)

                @pl.when(tp == 0)
                def _():
                    up_send[p, above, rows] = prod[p, above, rows].astype(BF16)

                up(p, above, i).start()

            @pl.when(falls)
            def _():
                @pl.when(tp < TP - 1)
                def _():
                    down(p, below, i).wait_recv()
                    dn_send[p, below, rows] = (prod[p, below, rows] + dn_recv[p, below, rows].astype(F32)).astype(BF16)

                @pl.when(tp == TP - 1)
                def _():
                    dn_send[p, below, rows] = prod[p, below, rows].astype(BF16)

                down(p, below, i).start()

    for one in AFTER:
        event(*one)

    @pl.loop(0, TP + 2)
    def _(step):
        for k, events in DURING.items():

            @pl.when((step == k) & (zh == 0))
            def _():
                for one in events:
                    event(*one)

        first = jnp.where(zh == 0, N - 1, jnp.minimum(TP - 1 - tp, tp + N))
        for p in range(PARTS):

            @pl.when(step == first)
            def _():
                for one in LAST[p]:
                    event(*one)

            chain(p, step)

    for p in range(PARTS):
        prod[p, tp] = product(p, tp)
    for inst in (KV, WA, WB, OA, OB):
        drain(inst)
    lsend.wait_send()
    for h in range(HEADS):
        oremote(h).wait_send()
    @pl.when(zh == 1)
    def _():
        drain(KVO)

    @pl.when(zh == 0)
    def _():
        remote(kbuf.at[zh, x, y], kbuf.at[zh, x, y], CROSS_K, zz).wait_send()
        remote(vbuf.at[zh, x, y], vbuf.at[zh, x, y], CROSS_V, zz).wait_send()

    cross(0).wait_send()
    cross(1).wait_send()
    remote(qbuf.at[c], qbuf.at[c], SIB_Q, sib).wait_send()


    def last(p):
        return remote(fsend.at[p], frecv.at[c, p], SIB_F + p, sib)

    for p in range(PARTS):
        for i in range(SUB):
            rows = sub(i)

            @pl.when(tp > 0)
            def _():
                up(p, tp, i).wait_recv()
                prod[p, tp, rows] += up_recv[p, tp, rows].astype(F32)

            @pl.when(tp < TP - 1)
            def _():
                down(p, tp, i).wait_recv()
                prod[p, tp, rows] += dn_recv[p, tp, rows].astype(F32)

            if i == 0:
                fsend[p] = prod[p, tp, rows].astype(BF16)
                last(p).start()
            else:
                frecv[c, p] = prod[p, tp, rows].astype(BF16)
    for p in range(PARTS):
        got(frecv.at[1 - c, p], SIB_F + p)
    for j in range(N):
        cols = slice(j * PIECE, (j + 1) * PIECE)
        out[:, j * 2 * WROWS : (j + 1) * 2 * WROWS] = jnp.concatenate(
            [frecv[k, p, :, cols] for k in range(2) for p in range(PARTS)], axis=1
        )

    for p in range(PARTS):
        last(p).wait_send()
    @pl.loop(0, TP - 1)
    def _(k):
        d = TP - 1 - k

        @pl.when(tp < d)
        def _():
            for p in range(PARTS):
                for i in range(SUB):
                    up(p, d, i).wait_send()

        @pl.when(tp > k)
        def _():
            for p in range(PARTS):
                for i in range(SUB):
                    down(p, k, i).wait_send()


def body(queries, keys, values, out_weight):
    slab = (2, N, N)
    sums = (PARTS, TP, BOTH, COLS)
    return pl.pallas_call(
        kernel,
        out_shape=jax.ShapeDtypeStruct((ROWS, TP * WROWS), BF16),
        in_specs=[pl.BlockSpec(memory_space=pl.ANY)] * 4,
        out_specs=pl.BlockSpec(memory_space=pltpu.VMEM),
        scratch_shapes=[
            pltpu.VMEM(slab + (ROWS, HD), BF16),
            pltpu.VMEM(slab + (ROWS, HD), BF16),
            pltpu.VMEM(slab + (WROWS, HEADS * HD), BF16),
            pltpu.VMEM((2, ROWS, HEADS * HD), BF16),
            pltpu.VMEM((HEADS, BOTH, HD), F32),
            pltpu.VMEM((HEADS, BOTH, HD), F32),
            pltpu.VMEM((HEADS, BOTH, HD), F32),
            pltpu.VMEM((HEADS, BOTH, HD), BF16),
            pltpu.VMEM((HEADS, BOTH, HD), BF16),
            pltpu.VMEM((BOTH, HD), F32),
            pltpu.VMEM((BOTH, HD), F32),
            pltpu.VMEM((BOTH, HEADS * HD), BF16),
            pltpu.VMEM(sums, BF16),
            pltpu.VMEM(sums, BF16),
            pltpu.VMEM(sums, BF16),
            pltpu.VMEM(sums, BF16),
            pltpu.VMEM(sums, F32),
            pltpu.VMEM((PARTS, ROWS, COLS), BF16),
            pltpu.VMEM((2, PARTS, ROWS, COLS), BF16),
            pltpu.SemaphoreType.DMA((SIB_F + PARTS,)),
            pltpu.SemaphoreType.DMA((SIB_F + PARTS,)),
            pltpu.SemaphoreType.DMA((PARTS, TP, SUB)),
            pltpu.SemaphoreType.DMA((PARTS, TP, SUB)),
            pltpu.SemaphoreType.DMA((PARTS, TP, SUB)),
            pltpu.SemaphoreType.DMA((PARTS, TP, SUB)),
            pltpu.SemaphoreType.DMA((4,)),
        ],
        compiler_params=pltpu.CompilerParams(
            collective_id=0, has_side_effects=True, vmem_limit_bytes=56 * 2**20
        ),
        cost_estimate=pl.CostEstimate(flops=5 * 10**9, bytes_accessed=2**20, transcendentals=0),
    )(queries, keys, values, out_weight)


def solution(mesh):
    return jax.shard_map(
        body,
        mesh=mesh,
        in_specs=(P("ctx", "tp"), P("ctx", "tp"), P("ctx", "tp"), P("ctx", "tp")),
        out_specs=P("ctx", "tp"),
        check_vma=False,
    )
```
